128 devices in a mesh: row: 8 (over y, z_hi), col: 16 (over x, z_lo, core).
Axes of the slice: x: 4, y: 4, z: 4 (z_hi: 2, z_lo: 2; z = z_hi * 2 + z_lo), core: 2. Of those that a mesh axis runs over, the one named last changes fastest.
Arguments:
- out_grad: bfloat16 [2048, 16384], P('col', 'row'), may hold values from -6 to 6
- codes: int32 [53248, 8192], P('col', 'row'), may hold values from 0 to 255
- scales: bfloat16 [416, 16384], P('col', 'row'), may hold values from 0.0007972717 to 0.0033874512
- activations: bfloat16 [2048, 53248], P('row', 'col'), may hold values from -6 to 6
- l_ff: bfloat16 [64, 53248], P(None, 'col'), may hold values from 0.099609375 to 1.8984375
- tenant_ids: int32 [2048], P('row'), may hold values from 0 to 63
Outputs:
- input_grad: bfloat16 [2048, 53248], P('row', 'col')
- tenant_grad: float32 [64, 53248], P('row', 'col')
The draws below stay inside these ranges and needn't reach their ends.
Inputs may be any that keep to these rules, and one draw needn't show every extreme that they name: Each word holds two codes as described in the reference program.
All inputs are finite; a program needn't handle non-finite values.
Results may differ from the reference program's by a relative error of at most 0.02.
Values may be sent and summed in bfloat16 or wider, within the bound.
No kernel may reach another device: no remote copies, remote signals or barrier semaphores. Data moves between devices by JAX's collectives and lax.ppermute only.
A program may use at most 256 MiB of HBM per device.

```python
import math
import jax
import jax.numpy as jnp
import numpy as np
from jax import lax

D = 16384
FF = 53248
GROUP = 128
TENANTS = 64
TOKENS = 2048
N_ROW = 8


def set_ends(array, key, low, largest):
    index_at = [jax.random.randint(jax.random.fold_in(key, axis), (), 0, length) for axis, length in enumerate(array.shape)]
    longest = array.shape.index(max(array.shape))
    next_to = index_at[:longest] + [(index_at[longest] + 1) % array.shape[longest]] + index_at[longest + 1:]
    return array.at[tuple(index_at)].set(low).at[tuple(next_to)].set(largest)


def levels(rng, shape, cuts, low, largest):
    level = 1.0
    for position, blocks in cuts:
        draws = jax.random.uniform(jax.random.fold_in(jax.random.fold_in(rng, 6), position), (blocks,), jnp.float32, low / len(cuts), largest / len(cuts))
        level = level * jnp.repeat(jnp.exp(draws), shape[position] // blocks).reshape((-1,) + (1,) * (len(shape) - 1 - position))
    return level


def rank_table(count, skew):
    portions = [(1 << 20) // math.isqrt(grade ** skew) + 1 for grade in range(1, count + 1)]
    spread = 1 + sum(portions) // (1 << 30)
    return np.cumsum(np.array([max(1, weight // spread) for weight in portions]))


def skewed_ids(stream_key, shape, amount, lean):
    grid = rank_table(amount, lean)
    pick = jax.random.randint(jax.random.fold_in(stream_key, 1), shape, 0, int(grid[amount - 1]))
    grade = jnp.searchsorted(jnp.asarray(grid, jnp.int32), pick, side="right")
    return jax.random.permutation(jax.random.fold_in(stream_key, 2), amount)[grade].astype(jnp.int32)


def noise(key, dims, scale, limit, cuts=(), kind=jnp.bfloat16):
    array = scale * jax.random.normal(key, dims, jnp.float32)
    if cuts:
        array = array * levels(key, dims, cuts, -0.22, 0.18)
    return jnp.clip(array, -limit, limit).astype(kind)


def setup_inputs(seed: int = 0) -> dict:
    seeds = jax.random.split(jax.random.key(seed), 7)
    return {
        "out_grad": noise(seeds[0], (TOKENS, D), 1.0, 6.0, ((0, 16), (1, 8))),
        "codes": set_ends(jax.random.randint(seeds[1], (FF, D // 2), 0, 256), jax.random.fold_in(seeds[1], 1), 0, 255).astype(jnp.int32),
        "scales": jnp.clip(jnp.exp(math.log(0.0033874512) - 1.4466375 * jax.random.uniform(seeds[2], (FF // GROUP, D), jnp.float32) ** levels(seeds[2], (FF // GROUP, D), ((0, 16), (1, 8)), -0.2, 0.2)), 0.0007972717, 0.0033874512).astype(jnp.bfloat16),
        "activations": noise(seeds[3], (TOKENS, FF), 1.0, 6.0, ((0, 8), (1, 16))),
        "l_ff": jnp.clip(1.0 + 0.18 * jax.random.normal(seeds[4], (TENANTS, FF), jnp.float32), 0.099609375, 1.8984375).astype(jnp.bfloat16),
        "tenant_ids": set_ends(skewed_ids(seeds[5], (TOKENS,), TENANTS, 1), jax.random.fold_in(seeds[5], 3), 0, TENANTS - 1).astype(jnp.int32),
    }


def unpack(packed):
    low_part = packed % 16
    high_part = packed // 16
    stacked = jnp.stack([low_part - 8, high_part - 8], axis=-1)
    return stacked.reshape(packed.shape[0], packed.shape[1] * 2)


def dequantize(packed, group_scales):
    values = unpack(packed).astype(jnp.float32)
    n_rows, n_cols = values.shape
    n_groups = group_scales.shape[0]
    scaled = values.reshape(n_groups, n_rows // n_groups, n_cols) * group_scales.astype(jnp.float32)[:, None, :]
    return scaled.reshape(n_rows, n_cols).astype(jnp.bfloat16)


def reference(out_grad, codes, scales, activations, l_ff, tenant_ids):
    width = D // N_ROW

    def block_step(carry, block):
        first = (block * width).astype(jnp.int32)
        packed = lax.dynamic_slice_in_dim(codes, (first // 2).astype(jnp.int32), width // 2, 1)
        group_scales = lax.dynamic_slice_in_dim(scales, first, width, 1)
        weight = dequantize(packed, group_scales)
        panel_rows = lax.dynamic_slice_in_dim(out_grad, first, width, 1)
        partial_value = jnp.dot(panel_rows, weight.T, preferred_element_type=jnp.float32).astype(jnp.bfloat16)
        return carry + partial_value.astype(jnp.float32), None

    start_grad = jnp.zeros((TOKENS, FF), jnp.float32)
    gradient, unused = lax.scan(block_step, start_grad, jnp.arange(N_ROW, dtype=jnp.int32))
    gains = l_ff.astype(jnp.float32)[tenant_ids]
    input_grad = (gradient * gains).astype(jnp.bfloat16)
    product = gradient * activations.astype(jnp.float32)
    tenant_grad = jax.ops.segment_sum(product, tenant_ids, num_segments=TENANTS)
    return input_grad, tenant_grad
```

```python
import functools

import jax
import jax.numpy as jnp
from jax import lax
from jax.experimental import pallas as pl
from jax.experimental.pallas import tpu as pltpu
from jax.sharding import PartitionSpec as P

TILE = 256
AHEAD = 5
F32 = jnp.float32
BF16 = jnp.bfloat16
PARTS = (32, 96)
GATHERS = (("a", 0, 0, 32), ("b", 1, 0, 32), ("c", 1, 32, 64))
CHUNKS = (
    (0, 32, True, "a", 0),
    (1, 32, True, "b", 0),
    (2, 32, False, "c", 0),
    (3, 32, True, "c", 32),
)
ORDER = ("a", "w", "b", "a", 0, "b", "c", 0, 1, 0, "c", 1, 2, 3, 0, 1, 3, 2, 1, 3, 2, 3, 2)


def place(x, y, z, core):
    x, y, z = x % 4, y % 4, z % 4
    return (y * 2 + z // 2) * 16 + x * 4 + (z % 2) * 2 + core


def route(move):
    return [
        (place(x, y, z, c), place(*move(x, y, z, c)))
        for x in range(4)
        for y in range(4)
        for z in range(4)
        for c in range(2)
    ]


def send(value, move):
    return lax.ppermute(value, ("row", "col"), route(move))


def y_up(x, y, z, c):
    return x, y + 1, z, c


def y_down(x, y, z, c):
    return x, y - 1, z, c


def z_across(x, y, z, c):
    return x, y, z + 2, c


def z_pair(x, y, z, c):
    return x, y, z + 1 - 2 * (z % 2), c


def x_up(x, y, z, c):
    return x + 1, y, z, c


def x_down(x, y, z, c):
    return x - 1, y, z, c


def x_across(x, y, z, c):
    return x + 2, y, z, c


def other_core(x, y, z, c):
    return x, y, z, 1 - c


def whole():
    return pl.BlockSpec(memory_space=pltpu.VMEM)


def anywhere():
    return pl.BlockSpec(memory_space=pl.ANY)


def chained(body, token, operands, in_specs, out_specs, out_shape, aliases=(), grid=(), scratch=(), mib=8, flops=1, name=""):
    n_in, n_out = len(in_specs), len(out_specs)

    def with_token(*refs):
        refs[n_in + 1 + n_out][...] = jnp.zeros((8, 128), F32)
        body(*refs[:n_in], *refs[n_in + 1 : n_in + 1 + n_out], *refs[n_in + 2 + n_out :])

    if grid:
        token_spec = pl.BlockSpec((8, 128), lambda i: (0, 0))
    else:
        token_spec = whole()
    *outs, token = pl.pallas_call(
        with_token,
        grid=grid,
        in_specs=[*in_specs, anywhere()],
        out_specs=[*out_specs, token_spec],
        out_shape=[*out_shape, jax.ShapeDtypeStruct((8, 128), F32)],
        scratch_shapes=scratch,
        input_output_aliases=dict(aliases),
        cost_estimate=pl.CostEstimate(flops=flops, bytes_accessed=1, transcendentals=0),
        compiler_params=pltpu.CompilerParams(vmem_limit_bytes=mib * 2**20),
        name=name,
    )(*operands, token)
    return outs, token


def split_body(x_ref, s_ref, s_out, *outs):
    into = lax.broadcasted_iota(jnp.int32, (256, 256), 0)
    col = lax.broadcasted_iota(jnp.int32, (256, 256), 1)
    pick = (into == jnp.where(col < 128, 2 * col, 2 * col - 255)).astype(BF16)
    for b in range(x_ref.shape[1] // 256):
        w = slice(256 * b, 256 * b + 256)
        x = jnp.dot(x_ref[:, w], pick, preferred_element_type=F32).astype(BF16)
        at = 0
        for out in outs:
            out[:, w] = x[at : at + out.shape[0]]
            at += out.shape[0]
        s_out[:, 0, w] = jnp.dot(s_ref[:, w], pick, preferred_element_type=F32)


def split_columns(x, scales, sizes):
    groups, k = scales.shape
    return chained(
        split_body,
        jnp.zeros((8, 128), F32),
        (x, scales),
        in_specs=[whole()] * 2,
        out_specs=[whole()] * (1 + len(sizes)),
        out_shape=[jax.ShapeDtypeStruct((groups, 1, k), F32)]
        + [jax.ShapeDtypeStruct((size, k), BF16) for size in sizes],
        name="split_columns",
    )


def join_body(rows, *refs):
    out, at = refs[-1], 0
    for (first, size), ref in zip(rows, refs):
        out[at : at + size] = ref[first : first + size]
        at += size


def join(token, *pieces):
    rows = tuple((first, size) for _, first, size in pieces)
    total, columns = sum(size for _, size in rows), pieces[0][0].shape[1]
    (out,), token = chained(
        functools.partial(join_body, rows),
        token,
        [array for array, _, _ in pieces],
        in_specs=[whole()] * len(pieces),
        out_specs=[whole()],
        out_shape=[jax.ShapeDtypeStruct((total, columns), BF16)],
        name="join",
    )
    return out, token


def dequantize_body(ahead, c_hbm, s_ref, w_hbm, c_v, w_v, c_sem, w_sem):
    tiles = c_hbm.shape[0]

    def fetch(i):
        at = lax.rem(i, ahead)
        return pltpu.make_async_copy(c_hbm.at[i], c_v.at[at], c_sem.at[at])

    def store(i):
        at = lax.rem(i, ahead)
        return pltpu.make_async_copy(w_v.at[at], w_hbm.at[i], w_sem.at[at])

    for i in range(ahead):
        fetch(i).start()

    def step(i, carry):
        at = lax.rem(i, ahead)
        fetch(i).wait()

        @pl.when(i >= ahead)
        def _():
            store(i - ahead).wait()

        for g in range(TILE // 128):
            rows = slice(128 * g, 128 * g + 128)
            for b in range(c_v.shape[2] // 128):
                q = c_v[at, rows, 128 * b : 128 * b + 128]
                scale = s_ref[TILE // 128 * i + g]
                for part, codes in enumerate((q & 15, q >> 4)):
                    cols = slice(256 * b + 128 * part, 256 * b + 128 * part + 128)
                    w = ((codes - 8).astype(F32) * scale[:, cols]).astype(BF16)
                    w_v[at, cols, rows] = w.T
        store(i).start()

        @pl.when(i + ahead < tiles)
        def _():
            fetch(i + ahead).start()

        return carry

    lax.fori_loop(0, tiles, step, 0)
    for i in range(tiles - ahead, tiles):
        store(i).wait()


def dequantize(token, codes, scales):
    ff, k = codes.shape
    tiles = ff // TILE
    (weight,), token = chained(
        functools.partial(dequantize_body, AHEAD),
        token,
        (codes.reshape(tiles, TILE, k), scales),
        in_specs=[anywhere(), whole()],
        out_specs=[anywhere()],
        out_shape=[jax.ShapeDtypeStruct((tiles, 2 * k, TILE), BF16)],
        scratch=[
            pltpu.VMEM((AHEAD, TILE, k), jnp.int32),
            pltpu.VMEM((AHEAD, 2 * k, TILE), BF16),
            pltpu.SemaphoreType.DMA((AHEAD,)),
            pltpu.SemaphoreType.DMA((AHEAD,)),
        ],
        mib=52,
        flops=11 * 10**9,
        name="dequantize",
    )
    return weight, token


def project_body(first, n, blocks, pieces, at_ref, mine, theirs, w_hbm, *refs):
    outs = refs[: len(pieces)]
    g_v, w_v, o_v, g_sem, w_sem, o_sem = refs[len(pieces) :]
    tiles, ring = w_hbm.shape[0], w_v.shape[0]
    ahead = 2

    def fetch(i):
        at = lax.rem(i, ring)
        return pltpu.make_async_copy(w_hbm.at[i], w_v.at[at], w_sem.at[at])

    def stores(i):
        at = pl.ds(pl.multiple_of(i * TILE, TILE), TILE)
        return [
            pltpu.make_async_copy(o_v.at[pl.ds(start, size), at], out.at[:, at], o_sem.at[p, i])
            for p, (out, (start, size)) in enumerate(zip(outs, pieces))
        ]

    y, z = lax.div(at_ref[0], 2), lax.rem(at_ref[0], 2)
    x, z_lo, core = lax.div(at_ref[1], 4), lax.rem(lax.div(at_ref[1], 2), 2), lax.rem(at_ref[1], 2)
    gathers = []
    for p, (dy, dz) in enumerate(blocks):
        to_y, to_z = lax.rem(y + dy, 4), lax.rem(z + dz, 2)
        block = lax.rem(to_y - x + 4, 4) * 2 + lax.rem(to_z + z_lo, 2)
        start = pl.multiple_of(block * (mine.shape[0] // 8) + first, 16)
        for other, source in enumerate((mine, theirs)):
            half = core if other == 0 else 1 - core
            at = pl.multiple_of((2 * p + half) * n, 16)
            gathers.append(
                pltpu.make_async_copy(
                    source.at[pl.ds(start, n), :],
                    g_v.at[pl.ds(at, n), :],
                    g_sem.at[2 * p + other],
                )
            )
    fetch(0).start()
    for copy in gathers:
        copy.start()
    fetch(1).start()
    for copy in gathers:
        copy.wait()

    def step(i, carry):
        fetch(i).wait()

        @pl.when(i + ahead < tiles)
        def _():
            fetch(i + ahead).start()

        at = pl.ds(pl.multiple_of(i * TILE, TILE), TILE)
        o_v[:, at] = jnp.dot(g_v[...], w_v[lax.rem(i, ring)], preferred_element_type=F32).astype(BF16)
        for copy in stores(i):
            copy.start()
        return carry

    lax.fori_loop(0, tiles, step, 0)

    def finish(i, carry):
        for copy in stores(i):
            copy.wait()
        return carry

    lax.fori_loop(0, tiles, finish, 0)


def project(token, here, mine, theirs, first, n, weight, blocks, pieces):
    tiles, k, _ = weight.shape
    ff = tiles * TILE
    return chained(
        functools.partial(project_body, first, n, blocks, pieces),
        token,
        (here, mine, theirs, weight),
        in_specs=[pl.BlockSpec(memory_space=pltpu.SMEM)] + [anywhere()] * 3,
        out_specs=[anywhere()] * len(pieces),
        out_shape=[jax.ShapeDtypeStruct((size, ff), BF16) for _, size in pieces],
        scratch=[
            pltpu.VMEM((16 * n, k), BF16),
            pltpu.VMEM((3, *weight.shape[1:]), BF16),
            pltpu.VMEM((16 * n, ff), BF16),
            pltpu.SemaphoreType.DMA((16,)),
            pltpu.SemaphoreType.DMA((3,)),
            pltpu.SemaphoreType.DMA((len(pieces), tiles)),
        ],
        mib=52,
        flops=4 * 16 * n * k * ff,
        name="project",
    )


STEPS = 2


def add_halves_body(up_ref, up_in, down_ref, down_in, up_out, down_out):
    up_out[...] = (up_ref[...].astype(F32) + up_in[...].astype(F32)).astype(BF16)
    down_out[...] = (down_ref[...].astype(F32) + down_in[...].astype(F32)).astype(BF16)


def add_halves(token, up, up_in, down, down_in):
    m, ff = up_in.shape
    low = pl.BlockSpec((m, ff // STEPS), lambda i: (0, i))
    high = pl.BlockSpec((m, ff // STEPS), lambda i: (1, i))
    return chained(
        add_halves_body,
        token,
        (up, up_in, down, down_in),
        grid=(STEPS,),
        in_specs=[low, low, high, low],
        out_specs=[low, high],
        out_shape=[jax.ShapeDtypeStruct(up.shape, BF16), jax.ShapeDtypeStruct(down.shape, BF16)],
        aliases={0: 0, 2: 1},
        name="add_halves",
    )


def sum_body(own_ref, up_ref, down_ref, keep_out, send_out):
    total = own_ref[...].astype(F32) + up_ref[...].astype(F32) + down_ref[...].astype(F32)
    m = keep_out.shape[0]
    keep_out[...] = total[:m]
    send_out[...] = total[m:].astype(BF16)


def sum_y(token, own, from_up, from_down):
    m2, ff = own.shape
    spec = pl.BlockSpec((m2, ff // STEPS), lambda i: (0, i))
    half = pl.BlockSpec((m2 // 2, ff // STEPS), lambda i: (0, i))
    return chained(
        sum_body,
        token,
        (own, from_up, from_down),
        grid=(STEPS,),
        in_specs=[spec] * 3,
        out_specs=[half] * 2,
        out_shape=[
            jax.ShapeDtypeStruct((m2 // 2, ff), F32),
            jax.ShapeDtypeStruct((m2 // 2, ff), BF16),
        ],
        name="sum_y",
    )


def sum_z_body(keep_ref, in_ref, *outs):
    at = 0
    for out in outs:
        rows = slice(at, at + out.shape[0])
        at += out.shape[0]
        out[...] = (keep_ref[rows].astype(F32) + in_ref[rows].astype(F32)).astype(out.dtype)


def sum_z(token, keep, arrived):
    m4, ff = keep.shape
    m = m4 // 4
    sizes = (m // 2, m // 2, m, m, m)
    spec = pl.BlockSpec((m4, ff // STEPS), lambda i: (0, i))
    return chained(
        sum_z_body,
        token,
        (keep, arrived),
        grid=(STEPS,),
        in_specs=[spec] * 2,
        out_specs=[pl.BlockSpec((size, ff // STEPS), lambda i: (0, i)) for size in sizes],
        out_shape=[jax.ShapeDtypeStruct((size, ff), BF16) for size in sizes],
        mib=12,
        name="sum_z",
    )


def finish_body(count, first, n, started, ids_ref, act_ref, l_ref, *refs):
    terms = refs[:count]
    out_ref, tenant_out = refs[-2:]
    gradient = terms[0][...].astype(F32)
    for term in terms[1:]:
        gradient = gradient + term[...].astype(F32)
    ids = jnp.concatenate([ids_ref[h : h + 1, first : first + n] for h in range(2)], axis=1)
    tenants = l_ref.shape[0]
    chosen = (ids == lax.broadcasted_iota(jnp.int32, (tenants, 2 * n), 0)).astype(BF16)
    gains = lax.dot_general(
        chosen, l_ref[...], (((0,), (0,)), ((), ())), preferred_element_type=F32
    )
    scaled = (gradient * gains).astype(BF16)
    total = None
    product = jnp.concatenate(
        [gradient[h * n : h * n + n] * act_ref[h].astype(F32) for h in range(2)], axis=0
    )
    coarse = product.astype(BF16)
    fine = (product - coarse.astype(F32)).astype(BF16)
    total = jnp.dot(chosen, coarse, preferred_element_type=F32) + jnp.dot(
        chosen, fine, preferred_element_type=F32
    )
    for h in range(2):
        out_ref[h] = scaled[h * n : h * n + n]
    if started:
        total = total + refs[count][...]
    tenant_out[...] = total.astype(tenant_out.dtype)


def finish(token, terms, first, n, ids, activations, l_ff, result, tenant_terms, last):
    tenants, ff = l_ff.shape
    wide = ff // STEPS
    started = tenant_terms is not None
    index = first // n
    rows = pl.BlockSpec((2, n, wide), lambda i: (0, index, i))
    flat = pl.BlockSpec((2 * n, wide), lambda i: (0, i))
    per_tenant = pl.BlockSpec((tenants, wide), lambda i: (0, i))
    operands = [ids, activations, l_ff, *terms]
    specs = [pl.BlockSpec(ids.shape, lambda i: (0, 0)), rows, per_tenant] + [flat] * len(terms)
    aliases = {}
    if started:
        if not last:
            aliases[len(operands)] = 1
        operands.append(tenant_terms)
        specs.append(per_tenant)
        aliases[len(operands)] = 0
        operands.append(result)
        specs.append(anywhere())
    return chained(
        functools.partial(finish_body, len(terms), first, n, started),
        token,
        operands,
        grid=(STEPS,),
        in_specs=specs,
        out_specs=[rows, per_tenant],
        out_shape=[
            jax.ShapeDtypeStruct(activations.shape, BF16),
            jax.ShapeDtypeStruct((tenants, ff), BF16 if last else F32),
        ],
        aliases=aliases,
        mib=14,
        name="finish",
    )


def gather_steps(part, paired, first, rows, kept):
    token = yield
    block, token = join(token, (part, first, rows), (paired, first, rows))
    token = yield token
    arrived = [send(block, move) for move in (x_down, x_across, x_up)]
    mine, token = join(token, *((array, 0, 2 * rows) for array in (block, *arrived)))
    kept.extend((mine, send(mine, other_core)))
    yield token


Y_BLOCKS = tuple((dy, dz) for dy in (2, 1, 3, 0) for dz in (0, 1))
Z_BLOCKS = tuple((dy, dz) for dz in (1, 0) for dy in (2, 1, 3, 0))


def chunk_steps(n, y_first, gathered, first, here, weights, tail):
    m = 2 * n
    token = yield
    if y_first:
        pieces = ((0, m), (m, m), (2 * m, 2 * m), (4 * m, 2 * m), (6 * m, 2 * m))
        (far_up, far_down, up, down, own), token = project(
            token, here, *gathered, first, n, *weights, Y_BLOCKS, pieces
        )
        token = yield token
        (up, down), token = add_halves(token, up, send(far_up, y_up), down, send(far_down, y_down))
        token = yield token
        (keep, leaves), token = sum_y(token, own, send(up, y_up), send(down, y_down))
        parts = (keep, send(leaves, z_across))
    else:
        pieces = ((0, 4 * m), (4 * m, 4 * m))
        (leaves, keep), token = project(
            token, here, *gathered, first, n, *weights, Z_BLOCKS, pieces
        )
        token = yield token
        (far_up, far_down, up, down, own), token = sum_z(token, keep, send(leaves, z_across))
        token = yield token
        (up, down), token = add_halves(token, up, send(far_up, y_up), down, send(far_down, y_down))
        parts = (own, send(up, y_up), send(down, y_down))
    token = yield token
    yield tail(token, parts)


def per_device(out_grad, codes, scales, activations, l_ff, tenant_ids):
    here = jnp.stack([lax.axis_index("row"), lax.axis_index("col")]).astype(jnp.int32)
    tokens, k = out_grad.shape
    ff = codes.shape[0]
    tenants = l_ff.shape[0]
    (split_scales, *parts), token = split_columns(out_grad, scales, PARTS)
    pairs = [(part, send(part, z_pair)) for part in parts]
    ids = tenant_ids.reshape(2, tokens)
    act = activations.reshape(2, tokens, ff)

    state = {"result": None, "terms": None}
    steps, kept, weights = {}, {}, []

    def weight_steps():
        token = yield
        weight, token = dequantize(token, codes, split_scales)
        weights.append(weight)
        yield token

    steps["w"] = weight_steps()
    for name, part, first, rows in GATHERS:
        kept[name] = []
        steps[name] = gather_steps(*pairs[part], first, rows, kept[name])
    first = 0
    for name, n, y_first, part, start in CHUNKS:

        def tail(token, terms, n=n, first=first, last=name == ORDER[-1]):
            (state["result"], state["terms"]), token = finish(
                token, terms, first, n, ids, act, l_ff, state["result"], state["terms"], last
            )
            return token

        steps[name] = chunk_steps(n, y_first, kept[part], start, here, weights, tail)
        first += n
    for generator in steps.values():
        next(generator)
    for name in ORDER:
        token = steps[name].send(token)
    n_row = lax.axis_size("row")
    terms, result = state["terms"], state["result"]
    arrived = lax.all_to_all(terms.reshape(n_row, tenants // n_row, ff), "row", 0, 0)
    tenant_grad = jnp.sum(arrived.astype(F32), axis=0)
    return result.reshape(2 * tokens, ff), tenant_grad


def solution(mesh):
    in_specs = (
        P("col", "row"),
        P("col", "row"),
        P("col", "row"),
        P("row", "col"),
        P(None, "col"),
        P("row"),
    )
    out_specs = (P("row", "col"), P("row", "col"))
    return jax.shard_map(
        per_device, mesh=mesh, in_specs=in_specs, out_specs=out_specs, check_vma=False
    )
```

```python
import functools

import jax
import jax.numpy as jnp
from jax import lax
from jax.experimental import pallas as pl
from jax.experimental.pallas import tpu as pltpu
from jax.sharding import PartitionSpec as P

TILE = 256
AHEAD = 5
F32 = jnp.float32
BF16 = jnp.bfloat16
PARTS = (32, 96)
GATHERS = (("a", 0, 0, 32, False), ("b", 1, 0, 96, True))
CHUNKS = (
    (0, 32, True, "a", 0),
    (1, 32, True, "b", 0),
    (2, 32, False, "b", 32),
    (3, 32, True, "b", 64),
)
ORDER = ("a", "w", "b", "a", 0, "b", 0, "b", 1, 0, 2, 1, 3, 0, 1, 3, 2, 1, 3, 2, 3, 2)


def place(x, y, z, core):
    x, y, z = x % 4, y % 4, z % 4
    return (y * 2 + z // 2) * 16 + x * 4 + (z % 2) * 2 + core


def route(move):
    return [
        (place(x, y, z, c), place(*move(x, y, z, c)))
        for x in range(4)
        for y in range(4)
        for z in range(4)
        for c in range(2)
    ]


def send(value, move):
    return lax.ppermute(value, ("row", "col"), route(move))


def y_up(x, y, z, c):
    return x, y + 1, z, c


def y_down(x, y, z, c):
    return x, y - 1, z, c


def z_across(x, y, z, c):
    return x, y, z + 2, c


def z_pair(x, y, z, c):
    return x, y, z + 1 - 2 * (z % 2), c


def x_up(x, y, z, c):
    return x + 1, y, z, c


def x_down(x, y, z, c):
    return x - 1, y, z, c


def x_across(x, y, z, c):
    return x + 2, y, z, c


def other_core(x, y, z, c):
    return x, y, z, 1 - c


def whole():
    return pl.BlockSpec(memory_space=pltpu.VMEM)


def anywhere():
    return pl.BlockSpec(memory_space=pl.ANY)


def chained(body, token, operands, in_specs, out_specs, out_shape, aliases=(), grid=(), scratch=(), mib=8, flops=1, name=""):
    n_in, n_out = len(in_specs), len(out_specs)

    def with_token(*refs):
        refs[n_in + 1 + n_out][...] = jnp.zeros((8, 128), F32)
        body(*refs[:n_in], *refs[n_in + 1 : n_in + 1 + n_out], *refs[n_in + 2 + n_out :])

    if grid:
        token_spec = pl.BlockSpec((8, 128), lambda i: (0, 0))
    else:
        token_spec = whole()
    *outs, token = pl.pallas_call(
        with_token,
        grid=grid,
        in_specs=[*in_specs, anywhere()],
        out_specs=[*out_specs, token_spec],
        out_shape=[*out_shape, jax.ShapeDtypeStruct((8, 128), F32)],
        scratch_shapes=scratch,
        input_output_aliases=dict(aliases),
        cost_estimate=pl.CostEstimate(flops=flops, bytes_accessed=1, transcendentals=0),
        compiler_params=pltpu.CompilerParams(vmem_limit_bytes=mib * 2**20),
        name=name,
    )(*operands, token)
    return outs, token


def split_body(x_ref, s_ref, s_out, *outs):
    into = lax.broadcasted_iota(jnp.int32, (256, 256), 0)
    col = lax.broadcasted_iota(jnp.int32, (256, 256), 1)
    pick = (into == jnp.where(col < 128, 2 * col, 2 * col - 255)).astype(BF16)
    for b in range(x_ref.shape[1] // 256):
        w = slice(256 * b, 256 * b + 256)
        x = jnp.dot(x_ref[:, w], pick, preferred_element_type=F32).astype(BF16)
        at = 0
        for out in outs:
            out[:, w] = x[at : at + out.shape[0]]
            at += out.shape[0]
        s_out[:, 0, w] = jnp.dot(s_ref[:, w], pick, preferred_element_type=F32)


def split_columns(x, scales, sizes):
    groups, k = scales.shape
    return chained(
        split_body,
        jnp.zeros((8, 128), F32),
        (x, scales),
        in_specs=[whole()] * 2,
        out_specs=[whole()] * (1 + len(sizes)),
        out_shape=[jax.ShapeDtypeStruct((groups, 1, k), F32)]
        + [jax.ShapeDtypeStruct((size, k), BF16) for size in sizes],
        name="split_columns",
    )


def join_body(rows, *refs):
    out, at = refs[-1], 0
    for (first, size), ref in zip(rows, refs):
        out[at : at + size] = ref[first : first + size]
        at += size


def join(token, *pieces):
    rows = tuple((first, size) for _, first, size in pieces)
    total, columns = sum(size for _, size in rows), pieces[0][0].shape[1]
    (out,), token = chained(
        functools.partial(join_body, rows),
        token,
        [array for array, _, _ in pieces],
        in_specs=[whole()] * len(pieces),
        out_specs=[whole()],
        out_shape=[jax.ShapeDtypeStruct((total, columns), BF16)],
        name="join",
    )
    return out, token


def dequantize_body(ahead, c_hbm, s_ref, w_hbm, c_v, w_v, c_sem, w_sem):
    tiles = c_hbm.shape[0]

    def fetch(i):
        at = lax.rem(i, ahead)
        return pltpu.make_async_copy(c_hbm.at[i], c_v.at[at], c_sem.at[at])

    def store(i):
        at = lax.rem(i, ahead)
        return pltpu.make_async_copy(w_v.at[at], w_hbm.at[i], w_sem.at[at])

    for i in range(ahead):
        fetch(i).start()

    def step(i, carry):
        at = lax.rem(i, ahead)
        fetch(i).wait()

        @pl.when(i >= ahead)
        def _():
            store(i - ahead).wait()

        for g in range(TILE // 128):
            rows = slice(128 * g, 128 * g + 128)
            for b in range(c_v.shape[2] // 128):
                q = c_v[at, rows, 128 * b : 128 * b + 128]
                scale = s_ref[TILE // 128 * i + g]
                for part, codes in enumerate((q & 15, q >> 4)):
                    cols = slice(256 * b + 128 * part, 256 * b + 128 * part + 128)
                    w = ((codes - 8).astype(F32) * scale[:, cols]).astype(BF16)
                    w_v[at, cols, rows] = w.T
        store(i).start()

        @pl.when(i + ahead < tiles)
        def _():
            fetch(i + ahead).start()

        return carry

    lax.fori_loop(0, tiles, step, 0)
    for i in range(tiles - ahead, tiles):
        store(i).wait()


def dequantize(token, codes, scales):
    ff, k = codes.shape
    tiles = ff // TILE
    (weight,), token = chained(
        functools.partial(dequantize_body, AHEAD),
        token,
        (codes.reshape(tiles, TILE, k), scales),
        in_specs=[anywhere(), whole()],
        out_specs=[anywhere()],
        out_shape=[jax.ShapeDtypeStruct((tiles, 2 * k, TILE), BF16)],
        scratch=[
            pltpu.VMEM((AHEAD, TILE, k), jnp.int32),
            pltpu.VMEM((AHEAD, 2 * k, TILE), BF16),
            pltpu.SemaphoreType.DMA((AHEAD,)),
            pltpu.SemaphoreType.DMA((AHEAD,)),
        ],
        mib=52,
        flops=11 * 10**9,
        name="dequantize",
    )
    return weight, token


def project_body(first, n, blocks, pieces, at_ref, mine, theirs, w_hbm, *refs):
    outs = refs[: len(pieces)]
    g_v, w_v, o_v, g_sem, w_sem, o_sem = refs[len(pieces) :]
    tiles, ring = w_hbm.shape[0], w_v.shape[0]
    ahead = 2

    def fetch(i):
        at = lax.rem(i, ring)
        return pltpu.make_async_copy(w_hbm.at[i], w_v.at[at], w_sem.at[at])

    def stores(i):
        at = pl.ds(pl.multiple_of(i * TILE, TILE), TILE)
        return [
            pltpu.make_async_copy(o_v.at[pl.ds(start, size), at], out.at[:, at], o_sem.at[p, i])
            for p, (out, (start, size)) in enumerate(zip(outs, pieces))
        ]

    y, z = lax.div(at_ref[0], 2), lax.rem(at_ref[0], 2)
    x, z_lo, core = lax.div(at_ref[1], 4), lax.rem(lax.div(at_ref[1], 2), 2), lax.rem(at_ref[1], 2)
    gathers = []
    for p, (dy, dz) in enumerate(blocks):
        to_y, to_z = lax.rem(y + dy, 4), lax.rem(z + dz, 2)
        block = lax.rem(to_y - x + 4, 4) * 2 + lax.rem(to_z + z_lo, 2)
        start = pl.multiple_of(block * (mine.shape[0] // 8) + first, 16)
        for other, source in enumerate((mine, theirs)):
            half = core if other == 0 else 1 - core
            at = pl.multiple_of((2 * p + half) * n, 16)
            gathers.append(
                pltpu.make_async_copy(
                    source.at[pl.ds(start, n), :],
                    g_v.at[pl.ds(at, n), :],
                    g_sem.at[2 * p + other],
                )
            )
    fetch(0).start()
    for copy in gathers:
        copy.start()
    fetch(1).start()
    for copy in gathers:
        copy.wait()

    def step(i, carry):
        fetch(i).wait()

        @pl.when(i + ahead < tiles)
        def _():
            fetch(i + ahead).start()

        at = pl.ds(pl.multiple_of(i * TILE, TILE), TILE)
        o_v[:, at] = jnp.dot(g_v[...], w_v[lax.rem(i, ring)], preferred_element_type=F32).astype(BF16)
        for copy in stores(i):
            copy.start()
        return carry

    lax.fori_loop(0, tiles, step, 0)

    def finish(i, carry):
        for copy in stores(i):
            copy.wait()
        return carry

    lax.fori_loop(0, tiles, finish, 0)


def project(token, here, mine, theirs, first, n, weight, blocks, pieces):
    tiles, k, _ = weight.shape
    ff = tiles * TILE
    return chained(
        functools.partial(project_body, first, n, blocks, pieces),
        token,
        (here, mine, theirs, weight),
        in_specs=[pl.BlockSpec(memory_space=pltpu.SMEM)] + [anywhere()] * 3,
        out_specs=[anywhere()] * len(pieces),
        out_shape=[jax.ShapeDtypeStruct((size, ff), BF16) for _, size in pieces],
        scratch=[
            pltpu.VMEM((16 * n, k), BF16),
            pltpu.VMEM((3, *weight.shape[1:]), BF16),
            pltpu.VMEM((16 * n, ff), BF16),
            pltpu.SemaphoreType.DMA((16,)),
            pltpu.SemaphoreType.DMA((3,)),
            pltpu.SemaphoreType.DMA((len(pieces), tiles)),
        ],
        mib=52,
        flops=4 * 16 * n * k * ff,
        name="project",
    )


STEPS = 2


def add_halves_body(up_ref, up_in, down_ref, down_in, up_out, down_out):
    up_out[...] = (up_ref[...].astype(F32) + up_in[...].astype(F32)).astype(BF16)
    down_out[...] = (down_ref[...].astype(F32) + down_in[...].astype(F32)).astype(BF16)


def add_halves(token, up, up_in, down, down_in):
    m, ff = up_in.shape
    low = pl.BlockSpec((m, ff // STEPS), lambda i: (0, i))
    high = pl.BlockSpec((m, ff // STEPS), lambda i: (1, i))
    return chained(
        add_halves_body,
        token,
        (up, up_in, down, down_in),
        grid=(STEPS,),
        in_specs=[low, low, high, low],
        out_specs=[low, high],
        out_shape=[jax.ShapeDtypeStruct(up.shape, BF16), jax.ShapeDtypeStruct(down.shape, BF16)],
        aliases={0: 0, 2: 1},
        name="add_halves",
    )


def sum_body(own_ref, up_ref, down_ref, keep_out, send_out):
    total = own_ref[...].astype(F32) + up_ref[...].astype(F32) + down_ref[...].astype(F32)
    m = keep_out.shape[0]
    keep_out[...] = total[:m]
    send_out[...] = total[m:].astype(BF16)


def sum_y(token, own, from_up, from_down):
    m2, ff = own.shape
    spec = pl.BlockSpec((m2, ff // STEPS), lambda i: (0, i))
    half = pl.BlockSpec((m2 // 2, ff // STEPS), lambda i: (0, i))
    return chained(
        sum_body,
        token,
        (own, from_up, from_down),
        grid=(STEPS,),
        in_specs=[spec] * 3,
        out_specs=[half] * 2,
        out_shape=[
            jax.ShapeDtypeStruct((m2 // 2, ff), F32),
            jax.ShapeDtypeStruct((m2 // 2, ff), BF16),
        ],
        name="sum_y",
    )


def sum_z_body(keep_ref, in_ref, *outs):
    at = 0
    for out in outs:
        rows = slice(at, at + out.shape[0])
        at += out.shape[0]
        out[...] = (keep_ref[rows].astype(F32) + in_ref[rows].astype(F32)).astype(out.dtype)


def sum_z(token, keep, arrived):
    m4, ff = keep.shape
    m = m4 // 4
    sizes = (m // 2, m // 2, m, m, m)
    spec = pl.BlockSpec((m4, ff // STEPS), lambda i: (0, i))
    return chained(
        sum_z_body,
        token,
        (keep, arrived),
        grid=(STEPS,),
        in_specs=[spec] * 2,
        out_specs=[pl.BlockSpec((size, ff // STEPS), lambda i: (0, i)) for size in sizes],
        out_shape=[jax.ShapeDtypeStruct((size, ff), BF16) for size in sizes],
        mib=12,
        name="sum_z",
    )


def finish_body(count, first, n, started, ids_ref, act_ref, l_ref, *refs):
    terms = refs[:count]
    out_ref, tenant_out = refs[-2:]
    gradient = terms[0][...].astype(F32)
    for term in terms[1:]:
        gradient = gradient + term[...].astype(F32)
    ids = jnp.concatenate([ids_ref[h : h + 1, first : first + n] for h in range(2)], axis=1)
    tenants = l_ref.shape[0]
    chosen = (ids == lax.broadcasted_iota(jnp.int32, (tenants, 2 * n), 0)).astype(BF16)
    gains = lax.dot_general(
        chosen, l_ref[...], (((0,), (0,)), ((), ())), preferred_element_type=F32
    )
    scaled = (gradient * gains).astype(BF16)
    total = None
    product = jnp.concatenate(
        [gradient[h * n : h * n + n] * act_ref[h].astype(F32) for h in range(2)], axis=0
    )
    coarse = product.astype(BF16)
    fine = (product - coarse.astype(F32)).astype(BF16)
    total = jnp.dot(chosen, coarse, preferred_element_type=F32) + jnp.dot(
        chosen, fine, preferred_element_type=F32
    )
    for h in range(2):
        out_ref[h] = scaled[h * n : h * n + n]
    if started:
        total = total + refs[count][...]
    tenant_out[...] = total.astype(tenant_out.dtype)


def finish(token, terms, first, n, ids, activations, l_ff, result, tenant_terms, last):
    tenants, ff = l_ff.shape
    wide = ff // STEPS
    started = tenant_terms is not None
    index = first // n
    rows = pl.BlockSpec((2, n, wide), lambda i: (0, index, i))
    flat = pl.BlockSpec((2 * n, wide), lambda i: (0, i))
    per_tenant = pl.BlockSpec((tenants, wide), lambda i: (0, i))
    operands = [ids, activations, l_ff, *terms]
    specs = [pl.BlockSpec(ids.shape, lambda i: (0, 0)), rows, per_tenant] + [flat] * len(terms)
    aliases = {}
    if started:
        if not last:
            aliases[len(operands)] = 1
        operands.append(tenant_terms)
        specs.append(per_tenant)
        aliases[len(operands)] = 0
        operands.append(result)
        specs.append(anywhere())
    return chained(
        functools.partial(finish_body, len(terms), first, n, started),
        token,
        operands,
        grid=(STEPS,),
        in_specs=specs,
        out_specs=[rows, per_tenant],
        out_shape=[
            jax.ShapeDtypeStruct(activations.shape, BF16),
            jax.ShapeDtypeStruct((tenants, ff), BF16 if last else F32),
        ],
        aliases=aliases,
        mib=14,
        name="finish",
    )


def gather_steps(part, paired, first, rows, relay, kept):
    token = yield
    block, token = join(token, (part, first, rows), (paired, first, rows))
    token = yield token
    above, below = send(block, x_down), send(block, x_up)
    if relay:
        low, token = join(token, (below, 0, rows))
        high, token = join(token, (above, rows, rows))
        token = yield token
        across = ((send(low, x_up), 0, rows), (send(high, x_down), 0, rows))
    else:
        across = ((send(block, x_across), 0, 2 * rows),)
    mine, token = join(
        token, (block, 0, 2 * rows), (above, 0, 2 * rows), *across, (below, 0, 2 * rows)
    )
    kept.extend((mine, send(mine, other_core)))
    yield token


Y_BLOCKS = tuple((dy, dz) for dy in (2, 1, 3, 0) for dz in (0, 1))
Z_BLOCKS = tuple((dy, dz) for dz in (1, 0) for dy in (2, 1, 3, 0))


def chunk_steps(n, y_first, gathered, first, here, weights, tail):
    m = 2 * n
    token = yield
    if y_first:
        pieces = ((0, m), (m, m), (2 * m, 2 * m), (4 * m, 2 * m), (6 * m, 2 * m))
        (far_up, far_down, up, down, own), token = project(
            token, here, *gathered, first, n, *weights, Y_BLOCKS, pieces
        )
        token = yield token
        (up, down), token = add_halves(token, up, send(far_up, y_up), down, send(far_down, y_down))
        token = yield token
        (keep, leaves), token = sum_y(token, own, send(up, y_up), send(down, y_down))
        parts = (keep, send(leaves, z_across))
    else:
        pieces = ((0, 4 * m), (4 * m, 4 * m))
        (leaves, keep), token = project(
            token, here, *gathered, first, n, *weights, Z_BLOCKS, pieces
        )
        token = yield token
        (far_up, far_down, up, down, own), token = sum_z(token, keep, send(leaves, z_across))
        token = yield token
        (up, down), token = add_halves(token, up, send(far_up, y_up), down, send(far_down, y_down))
        parts = (own, send(up, y_up), send(down, y_down))
    token = yield token
    yield tail(token, parts)


def per_device(out_grad, codes, scales, activations, l_ff, tenant_ids):
    here = jnp.stack([lax.axis_index("row"), lax.axis_index("col")]).astype(jnp.int32)
    tokens, k = out_grad.shape
    ff = codes.shape[0]
    tenants = l_ff.shape[0]
    (split_scales, *parts), token = split_columns(out_grad, scales, PARTS)
    pairs = [(part, send(part, z_pair)) for part in parts]
    ids = tenant_ids.reshape(2, tokens)
    act = activations.reshape(2, tokens, ff)

    state = {"result": None, "terms": None}
    steps, kept, weights = {}, {}, []

    def weight_steps():
        token = yield
        weight, token = dequantize(token, codes, split_scales)
        weights.append(weight)
        yield token

    steps["w"] = weight_steps()
    for name, part, first, rows, relay in GATHERS:
        kept[name] = []
        steps[name] = gather_steps(*pairs[part], first, rows, relay, kept[name])
    first = 0
    for name, n, y_first, part, start in CHUNKS:

        def tail(token, terms, n=n, first=first, last=name == ORDER[-1]):
            (state["result"], state["terms"]), token = finish(
                token, terms, first, n, ids, act, l_ff, state["result"], state["terms"], last
            )
            return token

        steps[name] = chunk_steps(n, y_first, kept[part], start, here, weights, tail)
        first += n
    for generator in steps.values():
        next(generator)
    for name in ORDER:
        token = steps[name].send(token)
    n_row = lax.axis_size("row")
    terms, result = state["terms"], state["result"]
    arrived = lax.all_to_all(terms.reshape(n_row, tenants // n_row, ff), "row", 0, 0)
    tenant_grad = jnp.sum(arrived.astype(F32), axis=0)
    return result.reshape(2 * tokens, ff), tenant_grad


def solution(mesh):
    in_specs = (
        P("col", "row"),
        P("col", "row"),
        P("col", "row"),
        P("row", "col"),
        P(None, "col"),
        P("row"),
    )
    out_specs = (P("row", "col"), P("row", "col"))
    return jax.shard_map(
        per_device, mesh=mesh, in_specs=in_specs, out_specs=out_specs, check_vma=False
    )
```

```python
import functools

import jax
import jax.numpy as jnp
from jax import lax
from jax.experimental import pallas as pl
from jax.experimental.pallas import tpu as pltpu
from jax.sharding import PartitionSpec as P

TILE = 256
AHEAD = 5
F32 = jnp.float32
BF16 = jnp.bfloat16
PARTS = (32, 96)
GATHERS = (("a", 0, 0, 32, False), ("b", 1, 0, 96, True))
CHUNKS = (
    (0, 32, True, "a", 0),
    (1, 32, True, "b", 0),
    (2, 32, False, "b", 32),
    (3, 32, True, "b", 64),
)
ORDER = ("a", "w", "b", "a", 0, "b", 0, "b", 1, 0, 2, 1, 3, 0, 1, 3, 2, 1, 3, 2, 3, 2)


def place(x, y, z, core):
    x, y, z = x % 4, y % 4, z % 4
    return (y * 2 + z // 2) * 16 + x * 4 + (z % 2) * 2 + core


def route(move):
    return [
        (place(x, y, z, c), place(*move(x, y, z, c)))
        for x in range(4)
        for y in range(4)
        for z in range(4)
        for c in range(2)
    ]


def send(value, move):
    return lax.ppermute(value, ("row", "col"), route(move))


def y_up(x, y, z, c):
    return x, y + 1, z, c


def y_down(x, y, z, c):
    return x, y - 1, z, c


def z_across(x, y, z, c):
    return x, y, z + 2, c


def z_pair(x, y, z, c):
    return x, y, z + 1 - 2 * (z % 2), c


def x_up(x, y, z, c):
    return x + 1, y, z, c


def x_down(x, y, z, c):
    return x - 1, y, z, c


def x_across(x, y, z, c):
    return x + 2, y, z, c


def other_core(x, y, z, c):
    return x, y, z, 1 - c


def whole():
    return pl.BlockSpec(memory_space=pltpu.VMEM)


def anywhere():
    return pl.BlockSpec(memory_space=pl.ANY)


def chained(body, token, operands, in_specs, out_specs, out_shape, aliases=(), grid=(), scratch=(), mib=8, flops=1, name=""):
    n_in, n_out = len(in_specs), len(out_specs)

    def with_token(*refs):
        refs[n_in + 1 + n_out][...] = jnp.zeros((8, 128), F32)
        body(*refs[:n_in], *refs[n_in + 1 : n_in + 1 + n_out], *refs[n_in + 2 + n_out :])

    if grid:
        token_spec = pl.BlockSpec((8, 128), lambda i: (0, 0))
    else:
        token_spec = whole()
    *outs, token = pl.pallas_call(
        with_token,
        grid=grid,
        in_specs=[*in_specs, anywhere()],
        out_specs=[*out_specs, token_spec],
        out_shape=[*out_shape, jax.ShapeDtypeStruct((8, 128), F32)],
        scratch_shapes=scratch,
        input_output_aliases=dict(aliases),
        cost_estimate=pl.CostEstimate(flops=flops, bytes_accessed=1, transcendentals=0),
        compiler_params=pltpu.CompilerParams(vmem_limit_bytes=mib * 2**20),
        name=name,
    )(*operands, token)
    return outs, token


def split_body(x_ref, s_ref, s_out, *outs):
    into = lax.broadcasted_iota(jnp.int32, (256, 256), 0)
    col = lax.broadcasted_iota(jnp.int32, (256, 256), 1)
    pick = (into == jnp.where(col < 128, 2 * col, 2 * col - 255)).astype(BF16)
    for b in range(x_ref.shape[1] // 256):
        w = slice(256 * b, 256 * b + 256)
        x = jnp.dot(x_ref[:, w], pick, preferred_element_type=F32).astype(BF16)
        at = 0
        for out in outs:
            out[:, w] = x[at : at + out.shape[0]]
            at += out.shape[0]
        s_out[:, 0, w] = jnp.dot(s_ref[:, w], pick, preferred_element_type=F32)


def split_columns(x, scales, sizes):
    groups, k = scales.shape
    return chained(
        split_body,
        jnp.zeros((8, 128), F32),
        (x, scales),
        in_specs=[whole()] * 2,
        out_specs=[whole()] * (1 + len(sizes)),
        out_shape=[jax.ShapeDtypeStruct((groups, 1, k), F32)]
        + [jax.ShapeDtypeStruct((size, k), BF16) for size in sizes],
        name="split_columns",
    )


def join_body(rows, *refs):
    out, at = refs[-1], 0
    for (first, size), ref in zip(rows, refs):
        out[at : at + size] = ref[first : first + size]
        at += size


def join(token, *pieces):
    rows = tuple((first, size) for _, first, size in pieces)
    total, columns = sum(size for _, size in rows), pieces[0][0].shape[1]
    (out,), token = chained(
        functools.partial(join_body, rows),
        token,
        [array for array, _, _ in pieces],
        in_specs=[whole()] * len(pieces),
        out_specs=[whole()],
        out_shape=[jax.ShapeDtypeStruct((total, columns), BF16)],
        name="join",
    )
    return out, token


def dequantize_body(ahead, c_hbm, s_ref, w_hbm, c_v, w_v, c_sem, w_sem):
    tiles = c_hbm.shape[0]

    def fetch(i):
        at = lax.rem(i, ahead)
        return pltpu.make_async_copy(c_hbm.at[i], c_v.at[at], c_sem.at[at])

    def store(i):
        at = lax.rem(i, ahead)
        return pltpu.make_async_copy(w_v.at[at], w_hbm.at[i], w_sem.at[at])

    for i in range(ahead):
        fetch(i).start()

    def step(i, carry):
        at = lax.rem(i, ahead)
        fetch(i).wait()

        @pl.when(i >= ahead)
        def _():
            store(i - ahead).wait()

        for g in range(TILE // 128):
            rows = slice(128 * g, 128 * g + 128)
            for b in range(c_v.shape[2] // 128):
                q = c_v[at, rows, 128 * b : 128 * b + 128]
                scale = s_ref[TILE // 128 * i + g]
                for part, codes in enumerate((q & 15, q >> 4)):
                    cols = slice(256 * b + 128 * part, 256 * b + 128 * part + 128)
                    w = ((codes - 8).astype(F32) * scale[:, cols]).astype(BF16)
                    w_v[at, cols, rows] = w.T
        store(i).start()

        @pl.when(i + ahead < tiles)
        def _():
            fetch(i + ahead).start()

        return carry

    lax.fori_loop(0, tiles, step, 0)
    for i in range(tiles - ahead, tiles):
        store(i).wait()


def dequantize(token, codes, scales):
    ff, k = codes.shape
    tiles = ff // TILE
    (weight,), token = chained(
        functools.partial(dequantize_body, AHEAD),
        token,
        (codes.reshape(tiles, TILE, k), scales),
        in_specs=[anywhere(), whole()],
        out_specs=[anywhere()],
        out_shape=[jax.ShapeDtypeStruct((tiles, 2 * k, TILE), BF16)],
        scratch=[
            pltpu.VMEM((AHEAD, TILE, k), jnp.int32),
            pltpu.VMEM((AHEAD, 2 * k, TILE), BF16),
            pltpu.SemaphoreType.DMA((AHEAD,)),
            pltpu.SemaphoreType.DMA((AHEAD,)),
        ],
        mib=52,
        flops=11 * 10**9,
        name="dequantize",
    )
    return weight, token


def project_body(first, n, blocks, pieces, at_ref, mine, theirs, w_hbm, *refs):
    outs = refs[: len(pieces)]
    g_v, w_v, o_v, g_sem, w_sem, o_sem = refs[len(pieces) :]
    tiles, ring = w_hbm.shape[0], w_v.shape[0]
    ahead = 2

    def fetch(i):
        at = lax.rem(i, ring)
        return pltpu.make_async_copy(w_hbm.at[i], w_v.at[at], w_sem.at[at])

    def stores(i):
        at = pl.ds(pl.multiple_of(i * TILE, TILE), TILE)
        return [
            pltpu.make_async_copy(o_v.at[pl.ds(start, size), at], out.at[:, at], o_sem.at[p])
            for p, (out, (start, size)) in enumerate(zip(outs, pieces))
        ]

    y, z = lax.div(at_ref[0], 2), lax.rem(at_ref[0], 2)
    x, z_lo, core = lax.div(at_ref[1], 4), lax.rem(lax.div(at_ref[1], 2), 2), lax.rem(at_ref[1], 2)
    gathers = []
    for p, (dy, dz) in enumerate(blocks):
        to_y, to_z = lax.rem(y + dy, 4), lax.rem(z + dz, 2)
        block = lax.rem(to_y - x + 4, 4) * 2 + lax.rem(to_z + z_lo, 2)
        start = pl.multiple_of(block * (mine.shape[0] // 8) + first, 16)
        for other, source in enumerate((mine, theirs)):
            half = core if other == 0 else 1 - core
            at = pl.multiple_of((2 * p + half) * n, 16)
            gathers.append(
                pltpu.make_async_copy(
                    source.at[pl.ds(start, n), :],
                    g_v.at[pl.ds(at, n), :],
                    g_sem,
                )
            )
    fetch(0).start()
    for copy in gathers:
        copy.start()
    fetch(1).start()
    pltpu.make_async_copy(g_v, g_v, g_sem).wait()

    def step(i, carry):
        fetch(i).wait()

        @pl.when(i + ahead < tiles)
        def _():
            fetch(i + ahead).start()

        at = pl.ds(pl.multiple_of(i * TILE, TILE), TILE)
        o_v[:, at] = jnp.dot(g_v[...], w_v[lax.rem(i, ring)], preferred_element_type=F32).astype(BF16)
        for copy in stores(i):
            copy.start()
        return carry

    lax.fori_loop(0, tiles, step, 0)

    for p, (out, (start, size)) in enumerate(zip(outs, pieces)):
        pltpu.make_async_copy(o_v.at[pl.ds(start, size)], out, o_sem.at[p]).wait()


def project(token, here, mine, theirs, first, n, weight, blocks, pieces):
    tiles, k, _ = weight.shape
    ff = tiles * TILE
    return chained(
        functools.partial(project_body, first, n, blocks, pieces),
        token,
        (here, mine, theirs, weight),
        in_specs=[pl.BlockSpec(memory_space=pltpu.SMEM)] + [anywhere()] * 3,
        out_specs=[anywhere()] * len(pieces),
        out_shape=[jax.ShapeDtypeStruct((size, ff), BF16) for _, size in pieces],
        scratch=[
            pltpu.VMEM((16 * n, k), BF16),
            pltpu.VMEM((3, *weight.shape[1:]), BF16),
            pltpu.VMEM((16 * n, ff), BF16),
            pltpu.SemaphoreType.DMA,
            pltpu.SemaphoreType.DMA((3,)),
            pltpu.SemaphoreType.DMA((len(pieces),)),
        ],
        mib=52,
        flops=4 * 16 * n * k * ff,
        name="project",
    )


STEPS = 2


def add_halves_body(up_ref, up_in, down_ref, down_in, up_out, down_out):
    up_out[...] = (up_ref[...].astype(F32) + up_in[...].astype(F32)).astype(BF16)
    down_out[...] = (down_ref[...].astype(F32) + down_in[...].astype(F32)).astype(BF16)


def add_halves(token, up, up_in, down, down_in):
    m, ff = up_in.shape
    low = pl.BlockSpec((m, ff // STEPS), lambda i: (0, i))
    high = pl.BlockSpec((m, ff // STEPS), lambda i: (1, i))
    return chained(
        add_halves_body,
        token,
        (up, up_in, down, down_in),
        grid=(STEPS,),
        in_specs=[low, low, high, low],
        out_specs=[low, high],
        out_shape=[jax.ShapeDtypeStruct(up.shape, BF16), jax.ShapeDtypeStruct(down.shape, BF16)],
        aliases={0: 0, 2: 1},
        name="add_halves",
    )


def sum_body(own_ref, up_ref, down_ref, keep_out, send_out):
    total = own_ref[...].astype(F32) + up_ref[...].astype(F32) + down_ref[...].astype(F32)
    m = keep_out.shape[0]
    keep_out[...] = total[:m]
    send_out[...] = total[m:].astype(BF16)


def sum_y(token, own, from_up, from_down):
    m2, ff = own.shape
    spec = pl.BlockSpec((m2, ff // STEPS), lambda i: (0, i))
    half = pl.BlockSpec((m2 // 2, ff // STEPS), lambda i: (0, i))
    return chained(
        sum_body,
        token,
        (own, from_up, from_down),
        grid=(STEPS,),
        in_specs=[spec] * 3,
        out_specs=[half] * 2,
        out_shape=[
            jax.ShapeDtypeStruct((m2 // 2, ff), F32),
            jax.ShapeDtypeStruct((m2 // 2, ff), BF16),
        ],
        name="sum_y",
    )


def sum_z_body(keep_ref, in_ref, *outs):
    at = 0
    for out in outs:
        rows = slice(at, at + out.shape[0])
        at += out.shape[0]
        out[...] = (keep_ref[rows].astype(F32) + in_ref[rows].astype(F32)).astype(out.dtype)


def sum_z(token, keep, arrived):
    m4, ff = keep.shape
    m = m4 // 4
    sizes = (m // 2, m // 2, m, m, m)
    spec = pl.BlockSpec((m4, ff // STEPS), lambda i: (0, i))
    return chained(
        sum_z_body,
        token,
        (keep, arrived),
        grid=(STEPS,),
        in_specs=[spec] * 2,
        out_specs=[pl.BlockSpec((size, ff // STEPS), lambda i: (0, i)) for size in sizes],
        out_shape=[jax.ShapeDtypeStruct((size, ff), BF16) for size in sizes],
        mib=12,
        name="sum_z",
    )


def finish_body(count, first, n, started, ids_ref, act_ref, l_ref, *refs):
    terms = refs[:count]
    out_ref, tenant_out = refs[-2:]
    gradient = terms[0][...].astype(F32)
    for term in terms[1:]:
        gradient = gradient + term[...].astype(F32)
    ids = jnp.concatenate([ids_ref[h : h + 1, first : first + n] for h in range(2)], axis=1)
    tenants = l_ref.shape[0]
    chosen = (ids == lax.broadcasted_iota(jnp.int32, (tenants, 2 * n), 0)).astype(BF16)
    gains = lax.dot_general(
        chosen, l_ref[...], (((0,), (0,)), ((), ())), preferred_element_type=F32
    )
    scaled = (gradient * gains).astype(BF16)
    total = None
    product = jnp.concatenate(
        [gradient[h * n : h * n + n] * act_ref[h].astype(F32) for h in range(2)], axis=0
    )
    coarse = product.astype(BF16)
    fine = (product - coarse.astype(F32)).astype(BF16)
    total = jnp.dot(chosen, coarse, preferred_element_type=F32) + jnp.dot(
        chosen, fine, preferred_element_type=F32
    )
    for h in range(2):
        out_ref[h] = scaled[h * n : h * n + n]
    if started:
        total = total + refs[count][...]
    tenant_out[...] = total.astype(tenant_out.dtype)


def finish(token, terms, first, n, ids, activations, l_ff, result, tenant_terms, last):
    tenants, ff = l_ff.shape
    wide = ff // STEPS
    started = tenant_terms is not None
    index = first // n
    rows = pl.BlockSpec((2, n, wide), lambda i: (0, index, i))
    flat = pl.BlockSpec((2 * n, wide), lambda i: (0, i))
    per_tenant = pl.BlockSpec((tenants, wide), lambda i: (0, i))
    operands = [ids, activations, l_ff, *terms]
    specs = [pl.BlockSpec(ids.shape, lambda i: (0, 0)), rows, per_tenant] + [flat] * len(terms)
    aliases = {}
    if started:
        if not last:
            aliases[len(operands)] = 1
        operands.append(tenant_terms)
        specs.append(per_tenant)
        aliases[len(operands)] = 0
        operands.append(result)
        specs.append(anywhere())
    return chained(
        functools.partial(finish_body, len(terms), first, n, started),
        token,
        operands,
        grid=(STEPS,),
        in_specs=specs,
        out_specs=[rows, per_tenant],
        out_shape=[
            jax.ShapeDtypeStruct(activations.shape, BF16),
            jax.ShapeDtypeStruct((tenants, ff), BF16 if last else F32),
        ],
        aliases=aliases,
        mib=14,
        name="finish",
    )


def gather_steps(part, paired, first, rows, relay, kept):
    token = yield
    block, token = join(token, (part, first, rows), (paired, first, rows))
    token = yield token
    above, below = send(block, x_down), send(block, x_up)
    if relay:
        low, token = join(token, (below, 0, rows))
        high, token = join(token, (above, rows, rows))
        token = yield token
        across = ((send(low, x_up), 0, rows), (send(high, x_down), 0, rows))
    else:
        across = ((send(block, x_across), 0, 2 * rows),)
    mine, token = join(
        token, (block, 0, 2 * rows), (above, 0, 2 * rows), *across, (below, 0, 2 * rows)
    )
    kept.extend((mine, send(mine, other_core)))
    yield token


Y_BLOCKS = tuple((dy, dz) for dy in (2, 1, 3, 0) for dz in (0, 1))
Z_BLOCKS = tuple((dy, dz) for dz in (1, 0) for dy in (2, 1, 3, 0))


def chunk_steps(n, y_first, gathered, first, here, weights, tail):
    m = 2 * n
    token = yield
    if y_first:
        pieces = ((0, m), (m, m), (2 * m, 2 * m), (4 * m, 2 * m), (6 * m, 2 * m))
        (far_up, far_down, up, down, own), token = project(
            token, here, *gathered, first, n, *weights, Y_BLOCKS, pieces
        )
        token = yield token
        (up, down), token = add_halves(token, up, send(far_up, y_up), down, send(far_down, y_down))
        token = yield token
        (keep, leaves), token = sum_y(token, own, send(up, y_up), send(down, y_down))
        parts = (keep, send(leaves, z_across))
    else:
        pieces = ((0, 4 * m), (4 * m, 4 * m))
        (leaves, keep), token = project(
            token, here, *gathered, first, n, *weights, Z_BLOCKS, pieces
        )
        token = yield token
        (far_up, far_down, up, down, own), token = sum_z(token, keep, send(leaves, z_across))
        token = yield token
        (up, down), token = add_halves(token, up, send(far_up, y_up), down, send(far_down, y_down))
        parts = (own, send(up, y_up), send(down, y_down))
    token = yield token
    yield tail(token, parts)


def per_device(out_grad, codes, scales, activations, l_ff, tenant_ids):
    here = jnp.stack([lax.axis_index("row"), lax.axis_index("col")]).astype(jnp.int32)
    tokens, k = out_grad.shape
    ff = codes.shape[0]
    tenants = l_ff.shape[0]
    (split_scales, *parts), token = split_columns(out_grad, scales, PARTS)
    pairs = [(part, send(part, z_pair)) for part in parts]
    ids = tenant_ids.reshape(2, tokens)
    act = activations.reshape(2, tokens, ff)

    state = {"result": None, "terms": None}
    steps, kept, weights = {}, {}, []

    def weight_steps():
        token = yield
        weight, token = dequantize(token, codes, split_scales)
        weights.append(weight)
        yield token

    steps["w"] = weight_steps()
    for name, part, first, rows, relay in GATHERS:
        kept[name] = []
        steps[name] = gather_steps(*pairs[part], first, rows, relay, kept[name])
    first = 0
    for name, n, y_first, part, start in CHUNKS:

        def tail(token, terms, n=n, first=first, last=name == ORDER[-1]):
            (state["result"], state["terms"]), token = finish(
                token, terms, first, n, ids, act, l_ff, state["result"], state["terms"], last
            )
            return token

        steps[name] = chunk_steps(n, y_first, kept[part], start, here, weights, tail)
        first += n
    for generator in steps.values():
        next(generator)
    for name in ORDER:
        token = steps[name].send(token)
    n_row = lax.axis_size("row")
    terms, result = state["terms"], state["result"]
    arrived = lax.all_to_all(terms.reshape(n_row, tenants // n_row, ff), "row", 0, 0)
    tenant_grad = jnp.sum(arrived.astype(F32), axis=0)
    return result.reshape(2 * tokens, ff), tenant_grad


def solution(mesh):
    in_specs = (
        P("col", "row"),
        P("col", "row"),
        P("col", "row"),
        P("row", "col"),
        P(None, "col"),
        P("row"),
    )
    out_specs = (P("row", "col"), P("row", "col"))
    return jax.shard_map(
        per_device, mesh=mesh, in_specs=in_specs, out_specs=out_specs, check_vma=False
    )
```
